32 devices in a mesh: query: 2 (over core), lib: 16 (over z, y, x).
Axes of the slice: x: 2, y: 2, z: 4, core: 2. Of those that a mesh axis runs over, the one named last changes fastest.
Arguments:
- queries: bfloat16 [1024, 2048], P(('query', 'lib')), may hold values from -64 to 64
- query_bucket: int32 [1024], P(('query', 'lib')), may hold values from 0 to 31, as said below
- library: bfloat16 [49152, 2048], P(('lib', 'query')), may hold values from -64 to 64
- library_time: bfloat16 [49152], P(('lib', 'query')), may hold values from 0 to 2
- library_bucket: int32 [49152], P(('lib', 'query')), may hold values from 0 to 31, as said below
Outputs:
- expected_spectra: bfloat16 [1024, 2048], P(('query', 'lib'))
- expected_time: float32 [1024], P(('query', 'lib'))
- log_evidence: float32 [1024], P(('query', 'lib'))
The draws below stay inside these ranges and needn't reach their ends.
Inputs may be any that keep to these rules, and one draw needn't show every extreme that they name: `query_bucket`: library entries whose bucket differs from a query's by at most one are that query's candidates; the queries held by the devices at index i of lib lie in buckets 2 i and 2 i + 1. `library_bucket`: the library entries of every device hold each of the 32 buckets exactly 3072 // 64 times.
All inputs are finite; a program needn't handle non-finite values.
Results may differ from the reference program's by a relative error of at most 0.003.
Values may be sent and summed in bfloat16 or wider, within the bound.
No kernel may reach another device: no remote copies, remote signals or barrier semaphores. Data moves between devices by JAX's collectives and lax.ppermute only.
A program may use at most 128 MiB of HBM per device.

```python
from functools import partial
import jax
import jax.numpy as jnp
from jax import lax

BINS = 2048
QUERY_DEV = 32
ENTRY_DEV = 3072
SHARPNESS = 448
BUCKETS = 32
QUERIES = 1024
ENTRIES = 49152
BLOCK_ROWS = 512
N_QUERY = 2
N_LIB = 16


def raw_row(base, index):
    return jnp.clip(jax.random.normal(jax.random.fold_in(base, index), (BINS,), jnp.float32), -5.0, 5.0)


def block_permutation(base, index):
    return jax.random.permutation(jax.random.fold_in(base, index), ENTRY_DEV // N_QUERY)


def entry_permutations(key):
    per_device = ENTRY_DEV // N_QUERY
    return jax.vmap(partial(block_permutation, jax.random.fold_in(key, 12)))(jnp.arange(ENTRIES // per_device))


def draw_query_bucket(key, part):
    positions = jnp.arange(QUERIES)
    column = positions // QUERY_DEV % N_LIB
    lower_upper = jax.random.randint(jax.random.fold_in(key, 11), (QUERIES,), 0, 2, dtype=jnp.int32)
    return (2 * column + lower_upper).astype(jnp.int32)


def draw_library_bucket(key, part):
    return (entry_permutations(key) % BUCKETS).reshape(ENTRIES).astype(jnp.int32)


def draw_library(key, part):
    library_base = jax.random.fold_in(key, 13)
    spectra_rows = jax.vmap(partial(raw_row, library_base))(jnp.arange(ENTRIES))
    return jnp.clip(spectra_rows, -64.0, 64.0).astype(jnp.bfloat16)


def draw_queries(key, part):
    query_base = jax.random.fold_in(key, 15)
    positions = jnp.arange(QUERIES)
    spectra_rows = jax.vmap(partial(raw_row, query_base))(positions)
    return jnp.clip(spectra_rows, -64.0, 64.0).astype(jnp.bfloat16)


def block_levels(rng, extent, cuts, low, largest):
    gain = 1.0
    for axis_at, blocks in cuts:
        heights = jax.random.uniform(jax.random.fold_in(jax.random.fold_in(rng, 6), axis_at), (blocks,), jnp.float32, low / len(cuts), largest / len(cuts))
        gain = gain * jnp.repeat(jnp.exp(heights), extent[axis_at] // blocks).reshape((-1,) + (1,) * (len(extent) - 1 - axis_at))
    return gain


def setup_inputs(seed: int = 0) -> dict:
    keys = jax.random.split(jax.random.key(seed), 6)
    queries = draw_queries(jax.random.fold_in(keys[5], 71), 0)
    query_bucket = draw_query_bucket(jax.random.fold_in(keys[5], 71), 0)
    library = draw_library(jax.random.fold_in(keys[5], 71), 0)
    library_time = jnp.clip(2.0 * jax.random.uniform(keys[3], (ENTRIES,), jnp.float32) ** block_levels(keys[3], (ENTRIES,), ((0, 32),), -0.2, 0.2), 0.0, 2.0).astype(jnp.bfloat16)
    library_bucket = draw_library_bucket(jax.random.fold_in(keys[5], 71), 0)
    return dict(queries=queries, query_bucket=query_bucket, library=library, library_time=library_time, library_bucket=library_bucket)


def entry_scale(spectra_rows):
    return lax.rsqrt(lax.optimization_barrier(jnp.mean(jnp.square(spectra_rows.astype(jnp.float32)), axis=1)) + 1e-06)

def reference(queries, query_bucket, library, library_time, library_bucket):
    library_scale = entry_scale(library)

    def one_block(inputs):
        query_block, block_bucket = inputs
        query_scale = entry_scale(query_block) * (SHARPNESS / BINS)
        products = lax.dot_general(query_block, library, (((1,), (1,)), ((), ())), preferred_element_type=jnp.float32)
        inside = jnp.abs(block_bucket[:, None] - library_bucket[None, :]) <= 1
        scores = jnp.where(inside, products * query_scale[:, None] * library_scale[None, :], -jnp.inf)
        maxima = lax.optimization_barrier(jnp.max(scores, axis=1))
        weights = jnp.exp(scores - maxima[:, None]).astype(jnp.bfloat16)
        totals = lax.optimization_barrier(jnp.sum(weights.astype(jnp.float32), axis=1))
        time_sum = jnp.dot(weights, library_time, preferred_element_type=jnp.float32)
        spectra_sum = jnp.dot(weights, library, preferred_element_type=jnp.float32)
        expected = (spectra_sum / totals[:, None]).astype(jnp.bfloat16)
        return (expected, time_sum / totals, maxima + jnp.log(totals))
    blocks = (queries.reshape(N_QUERY, BLOCK_ROWS, BINS), query_bucket.reshape(N_QUERY, BLOCK_ROWS))
    spectra, times, evidence = lax.map(one_block, blocks)
    return (spectra.reshape(QUERIES, BINS), times.reshape(QUERIES), evidence.reshape(QUERIES))
```

```python
import functools
import math

import jax
import jax.numpy as jnp
from jax import lax
from jax.experimental import pallas as pl
from jax.experimental.pallas import tpu as pltpu
from jax.sharding import PartitionSpec as P

SHARPNESS = 448
EPSILON = 1e-06
LANES = 128
LOG2E = math.log2(math.e)
LN2 = math.log(2.0)
FRACTION_BITS = 14
SUM_BITS = 16
LOW_BITS = 15
MASKED = -1e30
NT = (((1,), (1,)), ((), ()))
MIB = 1 << 20


def sort_kernel(per_bucket, chunk, bucket_ref, time_ref, library_ref, sorted_ref, aux_ref):
    count, bins = library_ref.shape
    buckets = count // per_bucket
    before = (
        lax.broadcasted_iota(jnp.int32, (LANES, LANES), 0)
        < lax.broadcasted_iota(jnp.int32, (LANES, LANES), 1)
    ).astype(jnp.bfloat16)
    bucket_ids = lax.broadcasted_iota(jnp.int32, (buckets, LANES), 0)
    seen = (per_bucket * lax.broadcasted_iota(jnp.int32, (buckets, 1), 0)).astype(jnp.float32)
    places = []
    for at in range(0, count, LANES):
        member = bucket_ref[:, at : at + LANES] == bucket_ids
        member32 = member.astype(jnp.float32)
        earlier = jnp.dot(
            member32.astype(jnp.bfloat16), before, preferred_element_type=jnp.float32
        )
        places.append(jnp.sum(member32 * (earlier + seen), axis=0, keepdims=True))
        seen = seen + jnp.sum(member32, axis=1, keepdims=True)
    place = jnp.concatenate(places, axis=1).astype(jnp.int32)
    time_rows = jnp.broadcast_to(time_ref[...], (8, count)).astype(jnp.bfloat16)
    for at in range(0, count, chunk):
        rows = at + lax.broadcasted_iota(jnp.int32, (chunk, count), 0)
        chosen = (rows == place).astype(jnp.float32).astype(jnp.bfloat16)
        entries = jnp.dot(chosen, library_ref[...], preferred_element_type=jnp.float32)
        sorted_ref[at : at + chunk, :] = entries.astype(jnp.bfloat16)
        times = lax.dot_general(time_rows, chosen, NT, preferred_element_type=jnp.float32)
        mean = jnp.sum(entries * entries, axis=1, keepdims=True) / bins
        scale = jnp.broadcast_to(lax.rsqrt(mean + EPSILON), (chunk, LANES)).T[:8]
        bucket = ((at + lax.broadcasted_iota(jnp.int32, (8, chunk), 1)) // per_bucket).astype(
            jnp.float32
        )
        which = lax.broadcasted_iota(jnp.int32, (8, chunk), 0)
        aux_ref[:, at : at + chunk] = jnp.where(
            which == 0, scale, jnp.where(which == 1, times, bucket)
        )


def sort_library(library, library_time, library_bucket, per_bucket):
    count, bins = library.shape
    chunk = min(256, count)
    return pl.pallas_call(
        functools.partial(sort_kernel, per_bucket, chunk),
        out_shape=(
            jax.ShapeDtypeStruct((count, bins), jnp.bfloat16),
            jax.ShapeDtypeStruct((8, count), jnp.float32),
        ),
        compiler_params=pltpu.CompilerParams(vmem_limit_bytes=48 * MIB),
        cost_estimate=pl.CostEstimate(
            flops=2 * count * count * bins, bytes_accessed=4 * count * bins, transcendentals=0
        ),
        name="sort_library",
    )(library_bucket.reshape(1, count), library_time.astype(jnp.float32).reshape(1, count), library)


def encode(out, rows, vector, k, total, time_sum):
    bins = vector.shape[1]
    largest = jnp.maximum(jnp.max(jnp.abs(vector), axis=1, keepdims=True), 1e-30)
    e = jnp.ceil(jnp.log2(largest))
    coded = jnp.floor(vector * jnp.exp2(FRACTION_BITS - e) + 0.5).astype(jnp.int32)
    out[rows, :bins] = coded.astype(jnp.int16)
    lane = lax.broadcasted_iota(jnp.int32, (vector.shape[0], LANES), 1)
    total = (total * (1 << SUM_BITS) + 0.5).astype(jnp.int32)
    time_sum = (time_sum * (1 << SUM_BITS) + 0.5).astype(jnp.int32)
    low = (1 << LOW_BITS) - 1
    stats = jnp.zeros((vector.shape[0], LANES), jnp.int32)
    for at, value in enumerate(
        (k.astype(jnp.int32), e.astype(jnp.int32), total >> LOW_BITS, total & low, time_sum >> LOW_BITS, time_sum & low)
    ):
        stats = jnp.where(lane == at, value, stats)
    out[rows, bins:] = stats.astype(jnp.int16)


def merged(parts):
    bins = parts[0].shape[1] - LANES
    stats = [p[:, bins:].astype(jnp.int32).astype(jnp.float32) for p in parts]
    ks = [s[:, 0:1] for s in stats]
    k = functools.reduce(jnp.maximum, ks)
    high = float(1 << LOW_BITS)
    unit = 1.0 / (1 << SUM_BITS)
    vector = total = time_sum = 0.0
    for part, s, own in zip(parts, stats, ks):
        shift = jnp.exp2(own - k)
        total = total + (s[:, 2:3] * high + s[:, 3:4]) * (shift * unit)
        time_sum = time_sum + (s[:, 4:5] * high + s[:, 5:6]) * (shift * unit)
        factor = jnp.exp2(own - k + s[:, 1:2] - FRACTION_BITS)
        vector = vector + part[:, :bins].astype(jnp.int32).astype(jnp.float32) * factor
    return vector, k, total, time_sum


def merge_kernel(pieces, *refs):
    *parts, = refs[: len(refs) - pieces]
    outs = refs[len(refs) - pieces :]
    rows = parts[0].shape[0] // pieces
    for at, out in enumerate(outs):
        own = [p[at * rows : (at + 1) * rows, :] for p in parts]
        encode(out, slice(None), *merged(own))


def merge(parts, pieces):
    rows, width = parts[0].shape
    out = jax.ShapeDtypeStruct((rows // pieces, width), jnp.int16)
    return pl.pallas_call(
        functools.partial(merge_kernel, pieces),
        out_shape=(out,) * pieces,
        compiler_params=pltpu.CompilerParams(vmem_limit_bytes=32 * MIB),
        cost_estimate=pl.CostEstimate(
            flops=8 * rows * width * len(parts), bytes_accessed=2 * rows * width * (len(parts) + 1), transcendentals=0
        ),
        name="merge",
    )(*parts)


def finish_kernel(*refs):
    *parts, spectra_ref, time_ref, evidence_ref = refs
    vector, k, total, time_sum = merged([p[...] for p in parts])
    spectra_ref[...] = (vector / total).astype(jnp.bfloat16)
    shape = (total.shape[0], LANES)
    time_ref[...] = jnp.broadcast_to(time_sum / total, shape).T[:1]
    evidence_ref[...] = jnp.broadcast_to(k * LN2 + jnp.log(total), shape).T[:1]


def finish(parts):
    rows, width = parts[0].shape
    spectra, time, evidence = pl.pallas_call(
        finish_kernel,
        out_shape=(
            jax.ShapeDtypeStruct((rows, width - LANES), jnp.bfloat16),
            jax.ShapeDtypeStruct((1, rows), jnp.float32),
            jax.ShapeDtypeStruct((1, rows), jnp.float32),
        ),
        compiler_params=pltpu.CompilerParams(vmem_limit_bytes=32 * MIB),
        name="finish",
    )(*parts)
    return spectra, time.reshape(rows), evidence.reshape(rows)


def match_kernel(window, per_bucket, shards, base_ref, *refs):
    queries, refs = refs[:4], refs[4:]
    libraries, refs = refs[:shards], refs[shards:]
    auxes, refs = refs[:shards], refs[shards:]
    outs, refs = refs[:4], refs[4:]
    held, stacked, arrived = refs
    step = pl.program_id(0)
    steps = pl.num_programs(0)
    rows, width = queries[0].shape
    bins = width - LANES
    count = libraries[0].shape[0]

    def first_row(at):
        quad = base_ref[0] ^ at
        start = (quad * 8 - 1) * per_bucket // LANES * LANES
        return pl.multiple_of(jnp.clip(start, 0, count - window), LANES)

    def copies(at, slot):
        start = first_row(at)
        return [
            pltpu.make_async_copy(
                library.at[pl.ds(start, window), :],
                held.at[slot, pl.ds(s * window, window), :],
                arrived.at[slot, s],
            )
            for s, library in enumerate(libraries)
        ]

    @pl.when(step == 0)
    def _():
        for c in copies(0, 0):
            c.start()

    slot = lax.rem(step, 2)

    @pl.when(step + 1 < steps)
    def _():
        for c in copies(step + 1, 1 - slot):
            c.start()

    for v, q in enumerate(queries):
        stacked[v * rows : (v + 1) * rows, :] = q[...]
    mine = stacked[:, :bins]
    mine32 = mine.astype(jnp.float32)
    mean = jnp.sum(mine32 * mine32, axis=1, keepdims=True) / bins
    query_scale = lax.rsqrt(mean + EPSILON) * (SHARPNESS / bins)
    query_bucket = stacked[:, bins:].astype(jnp.float32)[:, 0:1]
    start = first_row(step)
    aux = jnp.concatenate([a[:, pl.ds(start, window)] for a in auxes], axis=1)

    for c in copies(step, slot):
        c.wait()
    entries = held.at[slot]
    products = lax.dot_general(mine, entries[...], NT, preferred_element_type=jnp.float32)
    scores = products * query_scale * aux[0:1] * LOG2E
    inside = jnp.abs(query_bucket - aux[2:3]) <= 1.0
    scores = jnp.where(inside, scores, MASKED)
    k = jnp.ceil(jnp.max(scores, axis=1, keepdims=True))
    weights = jnp.exp2(scores - k)
    total = jnp.sum(weights, axis=1, keepdims=True)
    time_sum = jnp.sum(weights * aux[1:2], axis=1, keepdims=True)
    upper = weights.astype(jnp.bfloat16)
    lower = (weights - upper.astype(jnp.float32)).astype(jnp.bfloat16)
    both = jnp.concatenate([upper, lower], axis=0)
    sums = jnp.dot(both, entries[...], preferred_element_type=jnp.float32)
    vector = sums[: 4 * rows] + sums[4 * rows :]
    for v, out in enumerate(outs):
        part = slice(v * rows, (v + 1) * rows)
        encode(out, slice(None), vector[part], k[part], total[part], time_sum[part])


def match(base, queries, libraries, auxes, per_bucket, steps):
    rows, width = queries[0].shape
    rows //= steps
    bins = width - LANES
    count = libraries[0].shape[0]
    shards = len(libraries)
    starts = [max(0, (8 * q - 1) * per_bucket // LANES * LANES) for q in range(steps)]
    ends = [min(count, (8 * q + 9) * per_bucket) for q in range(steps)]
    window = min(count, max(-(-(e - s) // LANES) * LANES for s, e in zip(starts, ends)))
    block = pl.BlockSpec((rows, width), lambda q, base: (q, 0))
    whole = pl.BlockSpec((8, count), lambda q, base: (0, 0))
    work = 4 * rows * shards * window * bins
    return pl.pallas_call(
        functools.partial(match_kernel, window, per_bucket, shards),
        out_shape=(jax.ShapeDtypeStruct(queries[0].shape, jnp.int16),) * 4,
        grid_spec=pltpu.PrefetchScalarGridSpec(
            num_scalar_prefetch=1,
            grid=(steps,),
            in_specs=[block] * 4 + [pl.BlockSpec(memory_space=pl.ANY)] * shards + [whole] * shards,
            out_specs=[block] * 4,
            scratch_shapes=[
                pltpu.VMEM((2, shards * window, bins), jnp.bfloat16),
                pltpu.VMEM((4 * rows, width), jnp.bfloat16),
                pltpu.SemaphoreType.DMA((2, shards)),
            ],
        ),
        compiler_params=pltpu.CompilerParams(vmem_limit_bytes=48 * MIB),
        cost_estimate=pl.CostEstimate(
            flops=steps * 6 * work, bytes_accessed=steps * 2 * shards * window * bins, transcendentals=0
        ),
        name="match",
    )(base, *queries, *libraries, *auxes)


def per_device(shards, places, queries, query_bucket, library, library_time, library_bucket):
    own_rows, bins = queries.shape
    per_bucket = library.shape[0] // (2 * places)
    far = places // 4

    def both_axes(first, second):
        return [
            (c * places + i, c * places + (i ^ (second if c % 2 else first)))
            for c in range(shards)
            for i in range(places)
        ]

    def send(value, first, second):
        return lax.ppermute(value, ("query", "lib"), both_axes(first, second))

    def swap(value, distance):
        return lax.ppermute(value, "query", [(c, c ^ distance) for c in range(shards)])

    bucket_columns = jnp.broadcast_to(query_bucket.astype(jnp.bfloat16)[:, None], (own_rows, LANES))
    own = jnp.concatenate([queries, bucket_columns], axis=1)
    gathered = [own] + [send(own, 4 * z, 4 * z) for z in range(1, far)]
    entries, aux = sort_library(library, library_time, library_bucket, per_bucket)
    libraries = [entries] + [swap(entries, d) for d in range(1, shards)]
    auxes = [aux] + [swap(aux, d) for d in range(1, shards)]
    near = jnp.concatenate(gathered, axis=0)
    second = send(near, 2, 1)
    first = send(near, 1, 2)
    corner = send(second, 1, 2)

    base = (lax.axis_index("lib") // 4).astype(jnp.int32).reshape(1)
    part_near, part_second, part_first, part_corner = match(
        base, (near, second, first, corner), libraries, auxes, per_bucket, far
    )
    from_corner = send(part_corner, 1, 2)
    from_first = send(part_first, 1, 2)
    (part_second,) = merge([part_second, from_corner], 1)
    from_second = send(part_second, 2, 1)
    parts = merge([part_near, from_first, from_second], far)
    arrived = [parts[0]] + [send(parts[z], 4 * z, 4 * z) for z in range(1, far)]
    return finish(arrived)


def solution(mesh):
    placed = (
        P(("query", "lib"), None),
        P(("query", "lib")),
        P(("lib", "query"), None),
        P(("lib", "query")),
        P(("lib", "query")),
    )
    return jax.shard_map(
        functools.partial(per_device, mesh.shape["query"], mesh.shape["lib"]),
        mesh=mesh,
        in_specs=placed,
        out_specs=(P(("query", "lib"), None), P(("query", "lib")), P(("query", "lib"))),
        check_vma=False,
    )
```

```python
import functools
import math

import jax
import jax.numpy as jnp
from jax import lax
from jax.experimental import pallas as pl
from jax.experimental.pallas import tpu as pltpu
from jax.sharding import PartitionSpec as P

SHARPNESS = 448
EPSILON = 1e-06
LANES = 128
LOG2E = math.log2(math.e)
LN2 = math.log(2.0)
FRACTION_BITS = 14
SUM_BITS = 16
LOW_BITS = 15
MASKED = -1e30
OUTSIDE = 1e6
UNIT = 16
LARGEST = 8
SORT_MIB, MATCH_MIB, MERGE_MIB = 20, 20, 4
NT = (((1,), (1,)), ((), ()))
MIB = 1 << 20


def split3(value):
    pieces = []
    for _ in range(3):
        piece = value.astype(jnp.bfloat16)
        pieces.append(piece)
        value = value - piece.astype(jnp.float32)
    return pieces


def sort_kernel(buckets, bucket_ref, time_ref, library_ref, sorted_ref, first_ref):
    count, bins = library_ref.shape

    def earlier(n):
        order = [lax.broadcasted_iota(jnp.int32, (n, n), d) for d in range(2)]
        return (order[0] < order[1]).astype(jnp.float32).astype(jnp.bfloat16)

    member = (
        bucket_ref[...] == lax.broadcasted_iota(jnp.int32, (buckets, count), 0)
    ).astype(jnp.float32)
    member16 = member.astype(jnp.bfloat16)
    before = jnp.dot(member16, earlier(count), preferred_element_type=jnp.float32)
    lower = lax.dot_general(
        earlier(buckets), member16, (((0,), (0,)), ((), ())), preferred_element_type=jnp.float32
    )
    first = jnp.sum(lower, axis=1, keepdims=True)
    place = jnp.sum(member * (before + first), axis=0, keepdims=True).astype(jnp.int32)
    first_ref[...] = jnp.broadcast_to(first, (buckets, LANES)).astype(jnp.int32)
    chosen = (
        (lax.broadcasted_iota(jnp.int32, (count, count), 0) == place)
        .astype(jnp.float32)
        .astype(jnp.bfloat16)
    )

    entries = library_ref[...]
    wide = entries.astype(jnp.float32)
    scale = lax.rsqrt(jnp.sum(wide * wide, axis=1, keepdims=True) / bins + EPSILON)
    which = lax.broadcasted_iota(jnp.int32, (LANES, count), 0)
    facts = jnp.where(which == 0, time_ref[...], jnp.where(which == 1, bucket_ref[...].astype(jnp.float32), 0.0)).T
    lane = lax.broadcasted_iota(jnp.int32, (count, LANES), 1)
    for at, piece in enumerate(split3(scale)):
        facts = jnp.where(lane == 2 + at, piece.astype(jnp.float32), facts)
    sorted_ref[:, :bins] = jnp.dot(chosen, entries, preferred_element_type=jnp.float32).astype(
        jnp.bfloat16
    )
    sorted_ref[:, bins:] = jnp.dot(
        chosen, facts.astype(jnp.bfloat16), preferred_element_type=jnp.float32
    ).astype(jnp.bfloat16)


def sort_library(blocks, buckets, library, library_time, library_bucket):
    total, bins = library.shape
    count = total // blocks
    row = pl.BlockSpec((1, count), lambda n: (0, n))
    return pl.pallas_call(
        functools.partial(sort_kernel, buckets),
        out_shape=(
            jax.ShapeDtypeStruct((total, bins + LANES), jnp.bfloat16),
            jax.ShapeDtypeStruct((blocks * buckets, LANES), jnp.int32),
        ),
        grid=(blocks,),
        in_specs=[row, row, pl.BlockSpec((count, bins), lambda n: (n, 0))],
        out_specs=[
            pl.BlockSpec((count, bins + LANES), lambda n: (n, 0)),
            pl.BlockSpec((buckets, LANES), lambda n: (n, 0)),
        ],
        compiler_params=pltpu.CompilerParams(vmem_limit_bytes=SORT_MIB * MIB),
        cost_estimate=pl.CostEstimate(flops=5 * count * total * bins, bytes_accessed=(4 * total * bins) // 1, transcendentals=0),
        name="sort_library",
    )(library_bucket, library_time, library)


def encode(out, rows, vector, k, total, time_sum):
    bins = vector.shape[1]
    largest = jnp.maximum(jnp.max(jnp.abs(vector), axis=1, keepdims=True), 1e-30)
    e = jnp.ceil(jnp.log2(largest))
    coded = jnp.floor(vector * jnp.exp2(FRACTION_BITS - e) + 0.5).astype(jnp.int32)
    out[rows, :bins] = coded.astype(jnp.int16)
    lane = lax.broadcasted_iota(jnp.int32, (vector.shape[0], LANES), 1)
    total = (total * (1 << SUM_BITS) + 0.5).astype(jnp.int32)
    time_sum = (time_sum * (1 << SUM_BITS) + 0.5).astype(jnp.int32)
    low = (1 << LOW_BITS) - 1
    stats = jnp.zeros((vector.shape[0], LANES), jnp.int32)
    for at, value in enumerate(
        (k.astype(jnp.int32), e.astype(jnp.int32), total >> LOW_BITS, total & low, time_sum >> LOW_BITS, time_sum & low)
    ):
        stats = jnp.where(lane == at, value, stats)
    out[rows, bins:] = stats.astype(jnp.int16)


def merged(parts):
    bins = parts[0].shape[1] - LANES
    stats = [p[:, bins:].astype(jnp.int32).astype(jnp.float32) for p in parts]
    ks = [s[:, 0:1] for s in stats]
    k = functools.reduce(jnp.maximum, ks)
    high = float(1 << LOW_BITS)
    unit = 1.0 / (1 << SUM_BITS)
    vector = total = time_sum = 0.0
    for part, s, own in zip(parts, stats, ks):
        shift = jnp.exp2(own - k)
        total = total + (s[:, 2:3] * high + s[:, 3:4]) * (shift * unit)
        time_sum = time_sum + (s[:, 4:5] * high + s[:, 5:6]) * (shift * unit)
        factor = jnp.exp2(own - k + s[:, 1:2] - FRACTION_BITS)
        vector = vector + part[:, :bins].astype(jnp.int32).astype(jnp.float32) * factor
    return vector, k, total, time_sum


def merge_kernel(pieces, *refs):
    parts = refs[: len(refs) - pieces]
    outs = refs[len(refs) - pieces :]
    rows = parts[0].shape[0] // pieces
    for at, out in enumerate(outs):
        own = [p[at * rows : (at + 1) * rows, :] for p in parts]
        encode(out, slice(None), *merged(own))


def merge(parts, pieces):
    rows, width = parts[0].shape
    out = jax.ShapeDtypeStruct((rows // pieces, width), jnp.int16)
    return pl.pallas_call(
        functools.partial(merge_kernel, pieces),
        out_shape=(out,) * pieces,
        compiler_params=pltpu.CompilerParams(vmem_limit_bytes=MERGE_MIB * MIB),
        cost_estimate=pl.CostEstimate(flops=(8 * rows * width * len(parts)) // 1, bytes_accessed=(2 * rows * width * (len(parts) + 1)) // 1, transcendentals=0),
        name="merge",
    )(*parts)


def finish_kernel(*refs):
    *parts, spectra_ref, time_ref, evidence_ref = refs
    vector, k, total, time_sum = merged([p[...] for p in parts])
    spectra_ref[...] = (vector / total).astype(jnp.bfloat16)
    shape = (total.shape[0], LANES)
    time_ref[...] = jnp.broadcast_to(time_sum / total, shape).T[:1]
    evidence_ref[...] = jnp.broadcast_to(k * LN2 + jnp.log(total), shape).T[:1]


def finish(parts):
    rows, width = parts[0].shape
    spectra, time, evidence = pl.pallas_call(
        finish_kernel,
        out_shape=(
            jax.ShapeDtypeStruct((rows, width - LANES), jnp.bfloat16),
            jax.ShapeDtypeStruct((1, rows), jnp.float32),
            jax.ShapeDtypeStruct((1, rows), jnp.float32),
        ),
        compiler_params=pltpu.CompilerParams(vmem_limit_bytes=MERGE_MIB * MIB),
        name="finish",
    )(*parts)
    return spectra, time.reshape(rows), evidence.reshape(rows)


def window_kernel(shards, blocks, buckets, quad_ref, first_ref, *refs):
    libraries, refs, arrived = refs[:shards], refs[shards:-1], refs[-1]
    nears, seconds, helds, factses, parts = (refs[at :: 5] for at in range(5))
    count = libraries[0].shape[0] // blocks
    entries, width = helds[0].shape
    share = entries // shards

    def fetch(held, sem, library, begin, units, filled):
        def copy(size, done):
            pltpu.make_async_copy(
                library.at[pl.ds(pl.multiple_of((begin + done) * UNIT, UNIT), size * UNIT), :],
                held.at[pl.ds(pl.multiple_of((filled + done) * UNIT, UNIT), size * UNIT), :],
                sem,
            ).start()

        most = LARGEST
        while most * UNIT > count:
            most //= 2

        def large(i, carry):
            copy(most, i * most)
            return carry

        lax.fori_loop(0, units // most, large, 0)
        size = most // 2
        while size:

            @pl.when((units & size) != 0)
            def _(size=size):
                copy(size, units // (2 * size) * (2 * size))

            size //= 2

    filled = []
    for at, held in enumerate(helds):
        low = jnp.maximum(8 * quad_ref[at] - 1, 0)
        high = 8 * quad_ref[at] + 9
        for shard, library in enumerate(libraries):
            region, sem = held.at[shard * share : (shard + 1) * share, :], arrived.at[at, shard]
            there = jnp.int32(0)
            for n in range(blocks):
                row = (shard * blocks + n) * buckets
                start = first_ref[row + low]
                end = first_ref[row + jnp.minimum(high, buckets - 1)]
                end = jnp.where(high >= buckets, count, end)
                begin = start // UNIT
                units = (end + UNIT - 1) // UNIT - begin
                fetch(region, sem, library, n * (count // UNIT) + begin, units, there)
                there = there + units
            fetch(region, sem, library, 0, share // UNIT - there, there)
            filled.append(there)

    for at, held in enumerate(helds):
        queries = jnp.concatenate([nears[at][...], seconds[at][...]], axis=0)
        products, here = [], []
        for shard in range(shards):
            region = held.at[shard * share : (shard + 1) * share, :]
            pltpu.make_async_copy(region, region, arrived.at[at, shard]).wait()
            products.append(score(queries, region))
            row = lax.broadcasted_iota(jnp.int32, (1, share), 1)
            here.append(row - filled[at * shards + shard] * UNIT)
        columns = held[:, width - LANES :].astype(jnp.float32).T
        which = lax.broadcasted_iota(jnp.int32, (8, entries), 0)
        bucket = jnp.where(jnp.concatenate(here, axis=1) < 0, columns[1:2], OUTSIDE)
        scale = columns[2:3] + columns[3:4] + columns[4:5]
        facts = jnp.where(which == 0, columns[0:1], jnp.where(which == 1, bucket, scale))
        factses[at][...] = facts
        weigh(queries, jnp.concatenate(products, axis=1), facts, held, parts[at])


def rest_kernel(far_ref, held, facts_ref, part_ref):
    queries = far_ref[...]
    weigh(queries, score(queries, held), facts_ref[...], held, part_ref)


def score(queries, held):
    bins = queries.shape[1] - LANES
    return lax.dot_general(
        queries[:, :bins], held[:, :bins], NT, preferred_element_type=jnp.float32
    )


def weigh(queries, products, facts, held, part_ref):
    rows, width = queries.shape
    bins = width - LANES
    wide = queries[:, :bins].astype(jnp.float32)
    mean = jnp.sum(wide * wide, axis=1, keepdims=True) / bins
    query_scale = lax.rsqrt(mean + EPSILON) * (SHARPNESS / bins)
    query_bucket = queries[:, bins:].astype(jnp.float32)[:, 0:1]
    time, bucket, scale = facts[0:1], facts[1:2], facts[2:3]
    scores = products * query_scale * scale * LOG2E
    scores = jnp.where(jnp.abs(query_bucket - bucket) <= 1.0, scores, MASKED)
    k = jnp.ceil(jnp.max(scores, axis=1, keepdims=True))
    weights = jnp.exp2(scores - k)
    total = jnp.sum(weights, axis=1, keepdims=True)
    time_sum = jnp.sum(weights * time, axis=1, keepdims=True)
    upper = weights.astype(jnp.bfloat16)
    lower = (weights - upper.astype(jnp.float32)).astype(jnp.bfloat16)
    both = jnp.concatenate([upper, lower], axis=0)
    sums = jnp.dot(both, held[:, :bins], preferred_element_type=jnp.float32)
    encode(part_ref, slice(None), sums[:rows] + sums[rows:], k, total, time_sum)


def match_near(quad, firsts, near, second, libraries, per_bucket, blocks, buckets):
    quads = len(near)
    rows, width = near[0].shape
    bins = width - LANES
    shards = len(libraries)
    units = (10 * per_bucket + blocks * 2 * (UNIT - 1)) // UNIT
    entries = shards * (-(-units * UNIT // LANES) * LANES)
    vmem, smem = pl.BlockSpec(memory_space=pltpu.VMEM), pl.BlockSpec(memory_space=pltpu.SMEM)
    outs = (
        jax.ShapeDtypeStruct((entries, width), jnp.bfloat16),
        jax.ShapeDtypeStruct((8, entries), jnp.float32),
        jax.ShapeDtypeStruct((2 * rows, width), jnp.int16),
    )

    def kernel(quad_ref, first_ref, *refs):
        ins, rest = refs[: shards + 2 * quads], refs[shards + 2 * quads :]
        by_quad = []
        for at in range(quads):
            by_quad += ins[shards + 2 * at : shards + 2 * at + 2]
            by_quad += rest[3 * at : 3 * at + 3]
        window_kernel(shards, blocks, buckets, quad_ref, first_ref, *ins[:shards], *by_quad, rest[-1])

    results = pl.pallas_call(
        kernel,
        out_shape=outs * quads,
        in_specs=[smem, smem] + [pl.BlockSpec(memory_space=pl.ANY)] * shards + [vmem] * (2 * quads),
        out_specs=[vmem] * (3 * quads),
        scratch_shapes=[pltpu.SemaphoreType.DMA((quads, shards))],
        compiler_params=pltpu.CompilerParams(vmem_limit_bytes=MATCH_MIB * MIB),
        cost_estimate=pl.CostEstimate(
            flops=45 * quads * rows * entries * bins, bytes_accessed=2 * entries * width, transcendentals=0
        ),
        name="match_near",
    )(quad, firsts, *libraries, *[q for both in zip(near, second) for q in both])
    return [results[3 * at : 3 * at + 3] for at in range(quads)]


def match_far(far, held, facts):
    rows, width = far.shape
    return pl.pallas_call(
        rest_kernel,
        out_shape=jax.ShapeDtypeStruct((rows, width), jnp.int16),
        compiler_params=pltpu.CompilerParams(vmem_limit_bytes=MATCH_MIB * MIB),
        cost_estimate=pl.CostEstimate(flops=15 * rows * held.shape[0] * width, bytes_accessed=(2 * held.size) // 1, transcendentals=0),
        name="match_far",
    )(far, held, facts)


def per_device(shards, places, queries, query_bucket, library, library_time, library_bucket):
    own_rows, bins = queries.shape
    per_bucket = library.shape[0] // (2 * places)
    layers = places // 4
    quads = layers // shards
    buckets = 2 * places
    core = lax.axis_index("query")
    layer = lax.axis_index("lib") // 4

    def send(value, first, second):
        pairs = [
            (c * places + i, c * places + (i ^ (second if c % 2 else first)))
            for c in range(shards)
            for i in range(places)
        ]
        return lax.ppermute(value, ("query", "lib"), pairs)

    def layer_pairs(stream, distance):
        for s in range(shards):
            for i in range(places):
                worker, at = divmod(i // 4, quads)
                yield (s ^ distance) * places + i, worker * places + ((at ^ stream) + quads * s) * 4 + i % 4

    def spread(value, stream):
        return lax.ppermute(value, ("query", "lib"), list(layer_pairs(stream, 0)))

    def collect(value, stream, distance):
        return lax.ppermute(value, ("query", "lib"), [(b, a) for a, b in layer_pairs(stream, distance)])

    def swap(value, distance):
        return lax.ppermute(value, "query", [(c, c ^ distance) for c in range(shards)])

    blocks = 3
    rows = jnp.concatenate([queries] + [swap(queries, d) for d in range(1, shards)], axis=0)
    row_bucket = jnp.concatenate([query_bucket] + [swap(query_bucket, d) for d in range(1, shards)])
    bucket_columns = jnp.broadcast_to(row_bucket.astype(jnp.bfloat16)[:, None], (shards * own_rows, LANES))
    own = jnp.concatenate([rows, bucket_columns], axis=1)

    tie = lax.optimization_barrier
    near = [spread(own, at) for at in range(quads)]
    bucket_row = library_bucket.reshape(1, -1)
    time_row = library_time.astype(jnp.float32).reshape(1, -1)
    entries, firsts = sort_library(blocks, buckets, library, time_row, bucket_row)
    entries, firsts, near = tie((entries, firsts, near))
    libraries = [entries] + [swap(entries, d) for d in range(1, shards)]
    firsts = firsts[:, 0]
    firsts = jnp.concatenate([firsts] + [swap(firsts, d) for d in range(1, shards)])
    second = [send(n, 2, 1) for n in near]
    second, near = tie((second, near))
    wide = [jnp.concatenate(both, axis=0) for both in zip(near, second)]

    far = [send(w, 1, 2) for w in wide]
    quad = jnp.stack([core * quads + (at ^ (layer % quads)) for at in range(quads)]).astype(jnp.int32)
    matched = match_near(quad, firsts, near, second, libraries, per_bucket, blocks, buckets)
    far, matched = tie((far, matched))
    from_far = []
    for at, (held, facts, _) in enumerate(matched):
        from_far.append(send(match_far(far[at], held, facts), 1, 2))
    returned = []
    for at, (_, _, near_sums) in enumerate(matched):
        near_sums, second_sums = merge([near_sums, from_far[at]], 2)
        pieces = merge([near_sums, send(second_sums, 2, 1)], shards)
        returned += [collect(piece, at, d) for d, piece in enumerate(pieces)]
    return finish(returned)


def solution(mesh):
    placed = (
        P(("query", "lib"), None),
        P(("query", "lib")),
        P(("lib", "query"), None),
        P(("lib", "query")),
        P(("lib", "query")),
    )
    return jax.shard_map(
        functools.partial(per_device, mesh.shape["query"], mesh.shape["lib"]),
        mesh=mesh,
        in_specs=placed,
        out_specs=(P(("query", "lib"), None), P(("query", "lib")), P(("query", "lib"))),
        check_vma=False,
    )
```

```python
import functools
import math

import jax
import jax.numpy as jnp
from jax import lax
from jax.experimental import pallas as pl
from jax.experimental.pallas import tpu as pltpu
from jax.sharding import PartitionSpec as P

SHARPNESS = 448
EPSILON = 1e-06
LANES = 128
LOG2E = math.log2(math.e)
LN2 = math.log(2.0)
FRACTION_BITS = 14
SUM_BITS = 16
LOW_BITS = 15
MASKED = -1e30
OUTSIDE = 1e6
UNIT = 16
LARGEST = 8
SORT_MIB, MATCH_MIB, MERGE_MIB = 20, 20, 4
NT = (((1,), (1,)), ((), ()))
MIB = 1 << 20


def split3(value):
    pieces = []
    for _ in range(3):
        piece = value.astype(jnp.bfloat16)
        pieces.append(piece)
        value = value - piece.astype(jnp.float32)
    return pieces


def sort_kernel(buckets, time_ref, bucket_ref, library_ref, sorted_ref, first_ref, facts_ref):
    count, bins = library_ref.shape
    total = time_ref.shape[0]

    @pl.when(pl.program_id(0) == 0)
    def _():
        facts_ref[0:1, :] = time_ref[...].astype(jnp.float32).reshape(1, total)
        facts_ref[1:2, :] = bucket_ref[...].astype(jnp.float32).reshape(1, total)


    def earlier(n):
        order = [lax.broadcasted_iota(jnp.int32, (n, n), d) for d in range(2)]
        return (order[0] < order[1]).astype(jnp.float32).astype(jnp.bfloat16)

    here = pl.ds(pl.multiple_of(pl.program_id(0) * count, LANES), count)
    time, bucket = facts_ref[0:1, here], facts_ref[1:2, here]
    member = (
        bucket == lax.broadcasted_iota(jnp.int32, (buckets, count), 0).astype(jnp.float32)
    ).astype(jnp.float32)
    member16 = member.astype(jnp.bfloat16)
    before = jnp.dot(member16, earlier(count), preferred_element_type=jnp.float32)
    lower = lax.dot_general(
        earlier(buckets), member16, (((0,), (0,)), ((), ())), preferred_element_type=jnp.float32
    )
    first = jnp.sum(lower, axis=1, keepdims=True)
    place = jnp.sum(member * (before + first), axis=0, keepdims=True).astype(jnp.int32)
    first_ref[...] = jnp.broadcast_to(first, (buckets, LANES)).astype(jnp.int32)
    chosen = (
        (lax.broadcasted_iota(jnp.int32, (count, count), 0) == place)
        .astype(jnp.float32)
        .astype(jnp.bfloat16)
    )

    entries = library_ref[...]
    wide = entries.astype(jnp.float32)
    scale = lax.rsqrt(jnp.sum(wide * wide, axis=1, keepdims=True) / bins + EPSILON)
    which = lax.broadcasted_iota(jnp.int32, (LANES, count), 0)
    facts = jnp.where(which == 0, time, jnp.where(which == 1, bucket, 0.0)).T
    lane = lax.broadcasted_iota(jnp.int32, (count, LANES), 1)
    for at, piece in enumerate(split3(scale)):
        facts = jnp.where(lane == 2 + at, piece.astype(jnp.float32), facts)
    sorted_ref[:, :bins] = jnp.dot(chosen, entries, preferred_element_type=jnp.float32).astype(
        jnp.bfloat16
    )
    sorted_ref[:, bins:] = jnp.dot(
        chosen, facts.astype(jnp.bfloat16), preferred_element_type=jnp.float32
    ).astype(jnp.bfloat16)


def sort_library(blocks, buckets, library, library_time, library_bucket):
    total, bins = library.shape
    count = total // blocks
    return pl.pallas_call(
        functools.partial(sort_kernel, buckets),
        out_shape=(
            jax.ShapeDtypeStruct((total, bins + LANES), jnp.bfloat16),
            jax.ShapeDtypeStruct((blocks * buckets, LANES), jnp.int32),
        ),
        grid=(blocks,),
        in_specs=[
            pl.BlockSpec((total,), lambda n: (0,)),
            pl.BlockSpec((total,), lambda n: (0,)),
            pl.BlockSpec((count, bins), lambda n: (n, 0)),
        ],
        out_specs=[
            pl.BlockSpec((count, bins + LANES), lambda n: (n, 0)),
            pl.BlockSpec((buckets, LANES), lambda n: (n, 0)),
        ],
        scratch_shapes=[pltpu.VMEM((8, total), jnp.float32)],
        compiler_params=pltpu.CompilerParams(vmem_limit_bytes=SORT_MIB * MIB),
        cost_estimate=pl.CostEstimate(flops=5 * count * total * bins, bytes_accessed=4 * total * bins, transcendentals=0),
        name="sort_library",
    )(library_time, library_bucket, library)


def encode(out, rows, vector, k, total, time_sum):
    bins = vector.shape[1]
    largest = jnp.maximum(jnp.max(jnp.abs(vector), axis=1, keepdims=True), 1e-30)
    e = jnp.ceil(jnp.log2(largest))
    coded = jnp.floor(vector * jnp.exp2(FRACTION_BITS - e) + 0.5).astype(jnp.int32)
    out[rows, :bins] = coded.astype(jnp.int16)
    lane = lax.broadcasted_iota(jnp.int32, (vector.shape[0], LANES), 1)
    total = (total * (1 << SUM_BITS) + 0.5).astype(jnp.int32)
    time_sum = (time_sum * (1 << SUM_BITS) + 0.5).astype(jnp.int32)
    low = (1 << LOW_BITS) - 1
    stats = jnp.zeros((vector.shape[0], LANES), jnp.int32)
    for at, value in enumerate(
        (k.astype(jnp.int32), e.astype(jnp.int32), total >> LOW_BITS, total & low, time_sum >> LOW_BITS, time_sum & low)
    ):
        stats = jnp.where(lane == at, value, stats)
    out[rows, bins:] = stats.astype(jnp.int16)


def merged(parts):
    bins = parts[0].shape[1] - LANES
    stats = [p[:, bins:].astype(jnp.int32).astype(jnp.float32) for p in parts]
    ks = [s[:, 0:1] for s in stats]
    k = functools.reduce(jnp.maximum, ks)
    high = float(1 << LOW_BITS)
    unit = 1.0 / (1 << SUM_BITS)
    vector = total = time_sum = 0.0
    for part, s, own in zip(parts, stats, ks):
        shift = jnp.exp2(own - k)
        total = total + (s[:, 2:3] * high + s[:, 3:4]) * (shift * unit)
        time_sum = time_sum + (s[:, 4:5] * high + s[:, 5:6]) * (shift * unit)
        factor = jnp.exp2(own - k + s[:, 1:2] - FRACTION_BITS)
        vector = vector + part[:, :bins].astype(jnp.int32).astype(jnp.float32) * factor
    return vector, k, total, time_sum


def merge_kernel(pieces, *refs):
    parts = refs[: len(refs) - pieces]
    outs = refs[len(refs) - pieces :]
    rows = parts[0].shape[0] // pieces
    for at, out in enumerate(outs):
        own = [p[at * rows : (at + 1) * rows, :] for p in parts]
        encode(out, slice(None), *merged(own))


def merge(parts, pieces):
    rows, width = parts[0].shape
    out = jax.ShapeDtypeStruct((rows // pieces, width), jnp.int16)
    return pl.pallas_call(
        functools.partial(merge_kernel, pieces),
        out_shape=(out,) * pieces,
        compiler_params=pltpu.CompilerParams(vmem_limit_bytes=MERGE_MIB * MIB),
        cost_estimate=pl.CostEstimate(flops=8 * rows * width * len(parts), bytes_accessed=2 * rows * width * (len(parts) + 1), transcendentals=0),
        name="merge",
    )(*parts)


def finish_kernel(*refs):
    *parts, spectra_ref, time_ref, evidence_ref = refs
    vector, k, total, time_sum = merged([p[...] for p in parts])
    spectra_ref[...] = (vector / total).astype(jnp.bfloat16)
    shape = (total.shape[0], LANES)
    time_ref[...] = jnp.broadcast_to(time_sum / total, shape).T[:1]
    evidence_ref[...] = jnp.broadcast_to(k * LN2 + jnp.log(total), shape).T[:1]


def finish(parts):
    rows, width = parts[0].shape
    spectra, time, evidence = pl.pallas_call(
        finish_kernel,
        out_shape=(
            jax.ShapeDtypeStruct((rows, width - LANES), jnp.bfloat16),
            jax.ShapeDtypeStruct((1, rows), jnp.float32),
            jax.ShapeDtypeStruct((1, rows), jnp.float32),
        ),
        compiler_params=pltpu.CompilerParams(vmem_limit_bytes=MERGE_MIB * MIB),
        name="finish",
    )(*parts)
    return spectra, time.reshape(rows), evidence.reshape(rows)


def pack_kernel(*refs):
    *parts, out = refs
    count = len(parts) // 2
    rows, bins = parts[0].shape
    for d in range(count):
        at = slice(d * rows, (d + 1) * rows)
        out[at, :bins] = parts[d][...]
        bucket = parts[count + d][...].reshape(1, rows).astype(jnp.float32)
        if rows < LANES:
            bucket = jnp.concatenate([bucket, jnp.zeros((1, LANES - rows), jnp.float32)], axis=1)
        columns = jnp.broadcast_to(bucket, (LANES, LANES)).T
        out[at, bins:] = columns[:rows].astype(jnp.bfloat16)


def pack(queries, buckets):
    rows, bins = queries[0].shape
    return pl.pallas_call(
        pack_kernel,
        out_shape=jax.ShapeDtypeStruct((len(queries) * rows, bins + LANES), jnp.bfloat16),
        compiler_params=pltpu.CompilerParams(vmem_limit_bytes=MERGE_MIB * MIB),
        name="pack",
    )(*queries, *buckets)


def window_kernel(shards, blocks, buckets, quad_ref, first_ref, *refs):
    libraries, refs, arrived = refs[:shards], refs[shards:-1], refs[-1]
    nears, seconds, helds, factses, *parts = (refs[at :: 6] for at in range(6))
    count = libraries[0].shape[0] // blocks
    entries, width = helds[0].shape
    share = entries // shards

    def fetch(held, sem, library, begin, units, filled):
        def copy(size, done):
            pltpu.make_async_copy(
                library.at[pl.ds(pl.multiple_of((begin + done) * UNIT, UNIT), size * UNIT), :],
                held.at[pl.ds(pl.multiple_of((filled + done) * UNIT, UNIT), size * UNIT), :],
                sem,
            ).start()

        most = LARGEST
        while most * UNIT > count:
            most //= 2

        def large(i, carry):
            copy(most, i * most)
            return carry

        lax.fori_loop(0, units // most, large, 0)
        size = most // 2
        while size:

            @pl.when((units & size) != 0)
            def _(size=size):
                copy(size, units // (2 * size) * (2 * size))

            size //= 2

    filled = []
    for at, held in enumerate(helds):
        low = jnp.maximum(8 * quad_ref[at] - 1, 0)
        high = 8 * quad_ref[at] + 9
        for shard, library in enumerate(libraries):
            region, sem = held.at[shard * share : (shard + 1) * share, :], arrived.at[at, shard]
            there = jnp.int32(0)
            for n in range(blocks):
                row = (shard * blocks + n) * buckets
                start = first_ref[row + low]
                end = first_ref[row + jnp.minimum(high, buckets - 1)]
                end = jnp.where(high >= buckets, count, end)
                begin = start // UNIT
                units = (end + UNIT - 1) // UNIT - begin
                fetch(region, sem, library, n * (count // UNIT) + begin, units, there)
                there = there + units
            fetch(region, sem, library, 0, share // UNIT - there, there)
            filled.append(there)

    for at, held in enumerate(helds):
        queries = jnp.concatenate([nears[at][...], seconds[at][...]], axis=0)
        products, here = [], []
        for shard in range(shards):
            region = held.at[shard * share : (shard + 1) * share, :]
            pltpu.make_async_copy(region, region, arrived.at[at, shard]).wait()
            products.append(score(queries, region))
            row = lax.broadcasted_iota(jnp.int32, (1, share), 1)
            here.append(row - filled[at * shards + shard] * UNIT)
        columns = held[:, width - LANES :].astype(jnp.float32).T
        which = lax.broadcasted_iota(jnp.int32, (8, entries), 0)
        bucket = jnp.where(jnp.concatenate(here, axis=1) < 0, columns[1:2], OUTSIDE)
        scale = columns[2:3] + columns[3:4] + columns[4:5]
        facts = jnp.where(which == 0, columns[0:1], jnp.where(which == 1, bucket, scale))
        factses[at][...] = facts
        weigh(queries, jnp.concatenate(products, axis=1), facts, held, [p[at] for p in parts])


def rest_kernel(far_ref, held, facts_ref, *parts):
    queries = far_ref[...]
    weigh(queries, score(queries, held), facts_ref[...], held, parts)


def score(queries, held):
    bins = queries.shape[1] - LANES
    return lax.dot_general(
        queries[:, :bins], held[:, :bins], NT, preferred_element_type=jnp.float32
    )


def weigh(queries, products, facts, held, parts):
    rows, width = queries.shape
    bins = width - LANES
    wide = queries[:, :bins].astype(jnp.float32)
    mean = jnp.sum(wide * wide, axis=1, keepdims=True) / bins
    query_scale = lax.rsqrt(mean + EPSILON) * (SHARPNESS / bins)
    query_bucket = queries[:, bins:].astype(jnp.float32)[:, 0:1]
    time, bucket, scale = facts[0:1], facts[1:2], facts[2:3]
    scores = products * query_scale * scale * LOG2E
    scores = jnp.where(jnp.abs(query_bucket - bucket) <= 1.0, scores, MASKED)
    k = jnp.ceil(jnp.max(scores, axis=1, keepdims=True))
    weights = jnp.exp2(scores - k)
    total = jnp.sum(weights, axis=1, keepdims=True)
    time_sum = jnp.sum(weights * time, axis=1, keepdims=True)
    upper = weights.astype(jnp.bfloat16)
    lower = (weights - upper.astype(jnp.float32)).astype(jnp.bfloat16)
    both = jnp.concatenate([upper, lower], axis=0)
    sums = jnp.dot(both, held[:, :bins], preferred_element_type=jnp.float32)
    vector = sums[:rows] + sums[rows:]
    for n, part in enumerate(parts):
        at = slice(n * rows // len(parts), (n + 1) * rows // len(parts))
        encode(part, slice(None), vector[at], k[at], total[at], time_sum[at])


def match_near(quad, firsts, near, second, libraries, per_bucket, blocks, buckets):
    quads = len(near)
    rows, width = near[0].shape
    bins = width - LANES
    shards = len(libraries)
    units = (10 * per_bucket + blocks * 2 * (UNIT - 1)) // UNIT
    entries = shards * (-(-units * UNIT // LANES) * LANES)
    vmem, smem = pl.BlockSpec(memory_space=pltpu.VMEM), pl.BlockSpec(memory_space=pltpu.SMEM)
    outs = (
        jax.ShapeDtypeStruct((entries, width), jnp.bfloat16),
        jax.ShapeDtypeStruct((8, entries), jnp.float32),
        jax.ShapeDtypeStruct((rows, width), jnp.int16),
        jax.ShapeDtypeStruct((rows, width), jnp.int16),
    )

    def kernel(quad_ref, first_ref, *refs):
        ins, rest = refs[: shards + 2 * quads], refs[shards + 2 * quads :]
        by_quad = []
        for at in range(quads):
            by_quad += ins[shards + 2 * at : shards + 2 * at + 2]
            by_quad += rest[4 * at : 4 * at + 4]
        window_kernel(shards, blocks, buckets, quad_ref, first_ref, *ins[:shards], *by_quad, rest[-1])

    results = pl.pallas_call(
        kernel,
        out_shape=outs * quads,
        in_specs=[smem, smem] + [pl.BlockSpec(memory_space=pl.ANY)] * shards + [vmem] * (2 * quads),
        out_specs=[vmem] * (4 * quads),
        scratch_shapes=[pltpu.SemaphoreType.DMA((quads, shards))],
        compiler_params=pltpu.CompilerParams(vmem_limit_bytes=MATCH_MIB * MIB),
        cost_estimate=pl.CostEstimate(
            flops=45 * quads * rows * entries * bins, bytes_accessed=2 * entries * width, transcendentals=0
        ),
        name="match_near",
    )(quad, firsts, *libraries, *[q for both in zip(near, second) for q in both])
    return [results[4 * at : 4 * at + 4] for at in range(quads)]


def match_far(far, held, facts):
    rows, width = far.shape
    return pl.pallas_call(
        rest_kernel,
        out_shape=(jax.ShapeDtypeStruct((rows // 2, width), jnp.int16),) * 2,
        compiler_params=pltpu.CompilerParams(vmem_limit_bytes=MATCH_MIB * MIB),
        cost_estimate=pl.CostEstimate(flops=15 * rows * held.shape[0] * width, bytes_accessed=2 * held.size, transcendentals=0),
        name="match_far",
    )(far, held, facts)


def per_device(shards, places, queries, query_bucket, library, library_time, library_bucket):
    own_rows, bins = queries.shape
    per_bucket = library.shape[0] // (2 * places)
    layers = places // 4
    quads = layers // shards
    buckets = 2 * places
    core = lax.axis_index("query")
    layer = lax.axis_index("lib") // 4

    def send(value, first, second):
        pairs = [
            (c * places + i, c * places + (i ^ (second if c % 2 else first)))
            for c in range(shards)
            for i in range(places)
        ]
        return lax.ppermute(value, ("query", "lib"), pairs)

    def layer_pairs(stream, distance):
        for s in range(shards):
            for i in range(places):
                worker, at = divmod(i // 4, quads)
                yield (s ^ distance) * places + i, worker * places + ((at ^ stream) + quads * s) * 4 + i % 4

    def spread(value, stream):
        return lax.ppermute(value, ("query", "lib"), list(layer_pairs(stream, 0)))

    def collect(value, stream, distance):
        return lax.ppermute(value, ("query", "lib"), [(b, a) for a, b in layer_pairs(stream, distance)])

    def swap(value, distance):
        return lax.ppermute(value, "query", [(c, c ^ distance) for c in range(shards)])

    blocks = 3
    own = pack(
        [queries] + [swap(queries, d) for d in range(1, shards)],
        [query_bucket] + [swap(query_bucket, d) for d in range(1, shards)],
    )

    tie = lax.optimization_barrier
    near = [spread(own, at) for at in range(quads)]
    entries, firsts = sort_library(blocks, buckets, library, library_time, library_bucket)
    entries, firsts, near = tie((entries, firsts, near))
    libraries = [entries] + [swap(entries, d) for d in range(1, shards)]
    firsts = firsts[:, 0]
    firsts = jnp.concatenate([firsts] + [swap(firsts, d) for d in range(1, shards)])
    second = [send(n, 2, 1) for n in near]
    second, near = tie((second, near))
    wide = [jnp.concatenate(both, axis=0) for both in zip(near, second)]

    far = [send(w, 1, 2) for w in wide]
    quad = jnp.stack([core * quads + (at ^ (layer % quads)) for at in range(quads)]).astype(jnp.int32)
    matched = match_near(quad, firsts, near, second, libraries, per_bucket, blocks, buckets)
    far, matched = tie((far, matched))
    from_second = [send(second_sums, 2, 1) for _, _, _, second_sums in matched]
    first_sums, from_corner = [], []
    for at, (held, facts, _, _) in enumerate(matched):
        if at == quads - 1:
            far[at], from_second = tie((far[at], from_second))
        sums, corner_sums = match_far(far[at], held, facts)
        first_sums.append(sums)
        from_corner.append(send(corner_sums, 2, 1))
    returned = []
    for at, (_, _, near_sums, _) in enumerate(matched):
        (sums,) = merge([first_sums[at], from_corner[at]], 1)
        pieces = merge([near_sums, from_second[at], send(sums, 1, 2)], shards)
        returned += [collect(piece, at, d) for d, piece in enumerate(pieces)]
    return finish(returned)


def solution(mesh):
    placed = (
        P(("query", "lib"), None),
        P(("query", "lib")),
        P(("lib", "query"), None),
        P(("lib", "query")),
        P(("lib", "query")),
    )
    return jax.shard_map(
        functools.partial(per_device, mesh.shape["query"], mesh.shape["lib"]),
        mesh=mesh,
        in_specs=placed,
        out_specs=(P(("query", "lib"), None), P(("query", "lib")), P(("query", "lib"))),
        check_vma=False,
    )
```

```python
import functools
import math

import jax
import jax.numpy as jnp
from jax import lax
from jax.experimental import pallas as pl
from jax.experimental.pallas import tpu as pltpu
from jax.sharding import PartitionSpec as P

SHARPNESS = 448
EPSILON = 1e-06
LANES = 128
LOG2E = math.log2(math.e)
LN2 = math.log(2.0)
FRACTION_BITS = 14
SUM_BITS = 16
LOW_BITS = 15
MASKED = -1e30
OUTSIDE = 1e6
UNIT = 16
LARGEST = 8
SORT_MIB, MATCH_MIB, MERGE_MIB = 20, 20, 4
NT = (((1,), (1,)), ((), ()))
MIB = 1 << 20


def split3(value):
    pieces = []
    for _ in range(3):
        piece = value.astype(jnp.bfloat16)
        pieces.append(piece)
        value = value - piece.astype(jnp.float32)
    return pieces


def sort_kernel(buckets, time_ref, bucket_ref, library_ref, sorted_ref, first_ref, facts_ref):
    count, bins = library_ref.shape
    total = time_ref.shape[0]

    @pl.when(pl.program_id(0) == 0)
    def _():
        facts_ref[0:1, :] = time_ref[...].astype(jnp.float32).reshape(1, total)
        facts_ref[1:2, :] = bucket_ref[...].astype(jnp.float32).reshape(1, total)


    def earlier(n):
        order = [lax.broadcasted_iota(jnp.int32, (n, n), d) for d in range(2)]
        return (order[0] < order[1]).astype(jnp.float32).astype(jnp.bfloat16)

    here = pl.ds(pl.multiple_of(pl.program_id(0) * count, LANES), count)
    time, bucket = facts_ref[0:1, here], facts_ref[1:2, here]
    member = (
        bucket == lax.broadcasted_iota(jnp.int32, (buckets, count), 0).astype(jnp.float32)
    ).astype(jnp.float32)
    member16 = member.astype(jnp.bfloat16)
    before = jnp.dot(member16, earlier(count), preferred_element_type=jnp.float32)
    lower = lax.dot_general(
        earlier(buckets), member16, (((0,), (0,)), ((), ())), preferred_element_type=jnp.float32
    )
    first = jnp.sum(lower, axis=1, keepdims=True)
    place = jnp.sum(member * (before + first), axis=0, keepdims=True).astype(jnp.int32)
    first_ref[...] = jnp.broadcast_to(first, (buckets, LANES)).astype(jnp.int32)
    chosen = (
        (lax.broadcasted_iota(jnp.int32, (count, count), 0) == place)
        .astype(jnp.float32)
        .astype(jnp.bfloat16)
    )

    entries = library_ref[...]
    wide = entries.astype(jnp.float32)
    scale = lax.rsqrt(jnp.sum(wide * wide, axis=1, keepdims=True) / bins + EPSILON)
    which = lax.broadcasted_iota(jnp.int32, (LANES, count), 0)
    facts = jnp.where(which == 0, time, jnp.where(which == 1, bucket, 0.0)).T
    lane = lax.broadcasted_iota(jnp.int32, (count, LANES), 1)
    for at, piece in enumerate(split3(scale)):
        facts = jnp.where(lane == 2 + at, piece.astype(jnp.float32), facts)
    sorted_ref[:, :bins] = jnp.dot(chosen, entries, preferred_element_type=jnp.float32).astype(
        jnp.bfloat16
    )
    sorted_ref[:, bins:] = jnp.dot(
        chosen, facts.astype(jnp.bfloat16), preferred_element_type=jnp.float32
    ).astype(jnp.bfloat16)


def sort_library(blocks, buckets, library, library_time, library_bucket):
    total, bins = library.shape
    count = total // blocks
    return pl.pallas_call(
        functools.partial(sort_kernel, buckets),
        out_shape=(
            jax.ShapeDtypeStruct((total, bins + LANES), jnp.bfloat16),
            jax.ShapeDtypeStruct((blocks * buckets, LANES), jnp.int32),
        ),
        grid=(blocks,),
        in_specs=[
            pl.BlockSpec((total,), lambda n: (0,)),
            pl.BlockSpec((total,), lambda n: (0,)),
            pl.BlockSpec((count, bins), lambda n: (n, 0)),
        ],
        out_specs=[
            pl.BlockSpec((count, bins + LANES), lambda n: (n, 0)),
            pl.BlockSpec((buckets, LANES), lambda n: (n, 0)),
        ],
        scratch_shapes=[pltpu.VMEM((8, total), jnp.float32)],
        compiler_params=pltpu.CompilerParams(vmem_limit_bytes=SORT_MIB * MIB),
        cost_estimate=pl.CostEstimate(flops=5 * count * total * bins, bytes_accessed=4 * total * bins, transcendentals=0),
        name="sort_library",
    )(library_time, library_bucket, library)


def encode(out, rows, vector, k, total, time_sum):
    bins = vector.shape[1]
    largest = jnp.maximum(jnp.max(jnp.abs(vector), axis=1, keepdims=True), 1e-30)
    e = jnp.ceil(jnp.log2(largest))
    coded = jnp.floor(vector * jnp.exp2(FRACTION_BITS - e) + 0.5).astype(jnp.int32)
    out[rows, :bins] = coded.astype(jnp.int16)
    lane = lax.broadcasted_iota(jnp.int32, (vector.shape[0], LANES), 1)
    total = (total * (1 << SUM_BITS) + 0.5).astype(jnp.int32)
    time_sum = (time_sum * (1 << SUM_BITS) + 0.5).astype(jnp.int32)
    low = (1 << LOW_BITS) - 1
    stats = jnp.zeros((vector.shape[0], LANES), jnp.int32)
    for at, value in enumerate(
        (k.astype(jnp.int32), e.astype(jnp.int32), total >> LOW_BITS, total & low, time_sum >> LOW_BITS, time_sum & low)
    ):
        stats = jnp.where(lane == at, value, stats)
    out[rows, bins:] = stats.astype(jnp.int16)


def merged(parts):
    bins = parts[0].shape[1] - LANES
    stats = [p[:, bins:].astype(jnp.int32).astype(jnp.float32) for p in parts]
    ks = [s[:, 0:1] for s in stats]
    k = functools.reduce(jnp.maximum, ks)
    high = float(1 << LOW_BITS)
    unit = 1.0 / (1 << SUM_BITS)
    vector = total = time_sum = 0.0
    for part, s, own in zip(parts, stats, ks):
        shift = jnp.exp2(own - k)
        total = total + (s[:, 2:3] * high + s[:, 3:4]) * (shift * unit)
        time_sum = time_sum + (s[:, 4:5] * high + s[:, 5:6]) * (shift * unit)
        factor = jnp.exp2(own - k + s[:, 1:2] - FRACTION_BITS)
        vector = vector + part[:, :bins].astype(jnp.int32).astype(jnp.float32) * factor
    return vector, k, total, time_sum


def merge_kernel(pieces, *refs):
    parts = refs[: len(refs) - pieces]
    outs = refs[len(refs) - pieces :]
    rows = parts[0].shape[0] // pieces
    for at, out in enumerate(outs):
        own = [p[at * rows : (at + 1) * rows, :] for p in parts]
        encode(out, slice(None), *merged(own))


def merge(parts, pieces):
    rows, width = parts[0].shape
    out = jax.ShapeDtypeStruct((rows // pieces, width), jnp.int16)
    return pl.pallas_call(
        functools.partial(merge_kernel, pieces),
        out_shape=(out,) * pieces,
        compiler_params=pltpu.CompilerParams(vmem_limit_bytes=MERGE_MIB * MIB),
        cost_estimate=pl.CostEstimate(flops=8 * rows * width * len(parts), bytes_accessed=2 * rows * width * (len(parts) + 1), transcendentals=0),
        name="merge",
    )(*parts)


def finish_kernel(*refs):
    *parts, spectra_ref, time_ref, evidence_ref = refs
    vector, k, total, time_sum = merged([p[...] for p in parts])
    spectra_ref[...] = (vector / total).astype(jnp.bfloat16)
    shape = (total.shape[0], LANES)
    time_ref[...] = jnp.broadcast_to(time_sum / total, shape).T[:1]
    evidence_ref[...] = jnp.broadcast_to(k * LN2 + jnp.log(total), shape).T[:1]


def finish(parts):
    rows, width = parts[0].shape
    spectra, time, evidence = pl.pallas_call(
        finish_kernel,
        out_shape=(
            jax.ShapeDtypeStruct((rows, width - LANES), jnp.bfloat16),
            jax.ShapeDtypeStruct((1, rows), jnp.float32),
            jax.ShapeDtypeStruct((1, rows), jnp.float32),
        ),
        compiler_params=pltpu.CompilerParams(vmem_limit_bytes=MERGE_MIB * MIB),
        name="finish",
    )(*parts)
    return spectra, time.reshape(rows), evidence.reshape(rows)


def pack_kernel(*refs):
    *parts, out = refs
    count = len(parts) // 2
    rows, bins = parts[0].shape
    for d in range(count):
        at = slice(d * rows, (d + 1) * rows)
        out[at, :bins] = parts[d][...]
        bucket = parts[count + d][...].reshape(1, rows).astype(jnp.float32)
        if rows < LANES:
            bucket = jnp.concatenate([bucket, jnp.zeros((1, LANES - rows), jnp.float32)], axis=1)
        columns = jnp.broadcast_to(bucket, (LANES, LANES)).T
        out[at, bins:] = columns[:rows].astype(jnp.bfloat16)


def pack(queries, buckets):
    rows, bins = queries[0].shape
    return pl.pallas_call(
        pack_kernel,
        out_shape=jax.ShapeDtypeStruct((len(queries) * rows, bins + LANES), jnp.bfloat16),
        compiler_params=pltpu.CompilerParams(vmem_limit_bytes=MERGE_MIB * MIB),
        name="pack",
    )(*queries, *buckets)


def window_kernel(shards, blocks, buckets, quad_ref, first_ref, *refs):
    libraries, refs, arrived = refs[:shards], refs[shards:-1], refs[-1]
    nears, seconds, helds, factses, *parts = (refs[at :: 6] for at in range(6))
    count = libraries[0].shape[0] // blocks
    entries, width = helds[0].shape
    share = entries // shards

    def fetch(held, sem, library, begin, units, filled):
        def copy(size, done):
            pltpu.make_async_copy(
                library.at[pl.ds(pl.multiple_of((begin + done) * UNIT, UNIT), size * UNIT), :],
                held.at[pl.ds(pl.multiple_of((filled + done) * UNIT, UNIT), size * UNIT), :],
                sem,
            ).start()

        most = LARGEST
        while most * UNIT > count:
            most //= 2

        def large(i, carry):
            copy(most, i * most)
            return carry

        lax.fori_loop(0, units // most, large, 0)
        size = most // 2
        while size:

            @pl.when((units & size) != 0)
            def _(size=size):
                copy(size, units // (2 * size) * (2 * size))

            size //= 2

    filled = []
    for at, held in enumerate(helds):
        low = jnp.maximum(8 * quad_ref[at] - 1, 0)
        high = 8 * quad_ref[at] + 9
        for shard, library in enumerate(libraries):
            region, sem = held.at[shard * share : (shard + 1) * share, :], arrived.at[at, shard]
            there = jnp.int32(0)
            for n in range(blocks):
                row = (shard * blocks + n) * buckets
                start = first_ref[row + low]
                end = first_ref[row + jnp.minimum(high, buckets - 1)]
                end = jnp.where(high >= buckets, count, end)
                begin = start // UNIT
                units = (end + UNIT - 1) // UNIT - begin
                fetch(region, sem, library, n * (count // UNIT) + begin, units, there)
                there = there + units
            fetch(region, sem, library, 0, share // UNIT - there, there)
            filled.append(there)

    for at, held in enumerate(helds):
        queries = jnp.concatenate([nears[at][...], seconds[at][...]], axis=0)
        products, here = [], []
        for shard in range(shards):
            region = held.at[shard * share : (shard + 1) * share, :]
            pltpu.make_async_copy(region, region, arrived.at[at, shard]).wait()
            products.append(score(queries, region))
            row = lax.broadcasted_iota(jnp.int32, (1, share), 1)
            here.append(row - filled[at * shards + shard] * UNIT)
        columns = held[:, width - LANES :].astype(jnp.float32).T
        which = lax.broadcasted_iota(jnp.int32, (8, entries), 0)
        bucket = jnp.where(jnp.concatenate(here, axis=1) < 0, columns[1:2], OUTSIDE)
        scale = columns[2:3] + columns[3:4] + columns[4:5]
        facts = jnp.where(which == 0, columns[0:1], jnp.where(which == 1, bucket, scale))
        factses[at][...] = facts
        weigh(queries, jnp.concatenate(products, axis=1), facts, held, [p[at] for p in parts])


def rest_kernel(far_ref, held, facts_ref, *parts):
    queries = far_ref[...]
    weigh(queries, score(queries, held), facts_ref[...], held, parts)


def score(queries, held):
    bins = queries.shape[1] - LANES
    return lax.dot_general(
        queries[:, :bins], held[:, :bins], NT, preferred_element_type=jnp.float32
    )


def weigh(queries, products, facts, held, parts):
    rows, width = queries.shape
    bins = width - LANES
    wide = queries[:, :bins].astype(jnp.float32)
    mean = jnp.sum(wide * wide, axis=1, keepdims=True) / bins
    query_scale = lax.rsqrt(mean + EPSILON) * (SHARPNESS / bins)
    query_bucket = queries[:, bins:].astype(jnp.float32)[:, 0:1]
    time, bucket, scale = facts[0:1], facts[1:2], facts[2:3]
    scores = products * query_scale * scale * LOG2E
    scores = jnp.where(jnp.abs(query_bucket - bucket) <= 1.0, scores, MASKED)
    k = jnp.ceil(jnp.max(scores, axis=1, keepdims=True))
    weights = jnp.exp2(scores - k)
    total = jnp.sum(weights, axis=1, keepdims=True)
    time_sum = jnp.sum(weights * time, axis=1, keepdims=True)
    upper = weights.astype(jnp.bfloat16)
    lower = (weights - upper.astype(jnp.float32)).astype(jnp.bfloat16)
    both = jnp.concatenate([upper, lower], axis=0)
    sums = jnp.dot(both, held[:, :bins], preferred_element_type=jnp.float32)
    vector = sums[:rows] + sums[rows:]
    for n, part in enumerate(parts):
        at = slice(n * rows // len(parts), (n + 1) * rows // len(parts))
        encode(part, slice(None), vector[at], k[at], total[at], time_sum[at])


def match_near(quad, firsts, near, second, libraries, per_bucket, blocks, buckets):
    quads = len(near)
    rows, width = near[0].shape
    bins = width - LANES
    shards = len(libraries)
    units = (10 * per_bucket + blocks * 2 * (UNIT - 1)) // UNIT
    entries = shards * (-(-units * UNIT // LANES) * LANES)
    vmem, smem = pl.BlockSpec(memory_space=pltpu.VMEM), pl.BlockSpec(memory_space=pltpu.SMEM)
    outs = (
        jax.ShapeDtypeStruct((entries, width), jnp.bfloat16),
        jax.ShapeDtypeStruct((8, entries), jnp.float32),
        jax.ShapeDtypeStruct((rows, width), jnp.int16),
        jax.ShapeDtypeStruct((rows, width), jnp.int16),
    )

    def kernel(quad_ref, first_ref, *refs):
        ins, rest = refs[: shards + 2 * quads], refs[shards + 2 * quads :]
        by_quad = []
        for at in range(quads):
            by_quad += ins[shards + 2 * at : shards + 2 * at + 2]
            by_quad += rest[4 * at : 4 * at + 4]
        window_kernel(shards, blocks, buckets, quad_ref, first_ref, *ins[:shards], *by_quad, rest[-1])

    results = pl.pallas_call(
        kernel,
        out_shape=outs * quads,
        in_specs=[smem, smem] + [pl.BlockSpec(memory_space=pl.ANY)] * shards + [vmem] * (2 * quads),
        out_specs=[vmem] * (4 * quads),
        scratch_shapes=[pltpu.SemaphoreType.DMA((quads, shards))],
        compiler_params=pltpu.CompilerParams(vmem_limit_bytes=MATCH_MIB * MIB),
        cost_estimate=pl.CostEstimate(
            flops=45 * quads * rows * entries * bins, bytes_accessed=2 * entries * width, transcendentals=0
        ),
        name="match_near",
    )(quad, firsts, *libraries, *[q for both in zip(near, second) for q in both])
    return [results[4 * at : 4 * at + 4] for at in range(quads)]


def match_far(far, held, facts):
    rows, width = far.shape
    return pl.pallas_call(
        rest_kernel,
        out_shape=(jax.ShapeDtypeStruct((rows // 2, width), jnp.int16),) * 2,
        compiler_params=pltpu.CompilerParams(vmem_limit_bytes=MATCH_MIB * MIB),
        cost_estimate=pl.CostEstimate(flops=15 * rows * held.shape[0] * width, bytes_accessed=2 * held.size, transcendentals=0),
        name="match_far",
    )(far, held, facts)


def per_device(shards, places, queries, query_bucket, library, library_time, library_bucket):
    own_rows, bins = queries.shape
    per_bucket = library.shape[0] // (2 * places)
    layers = places // 4
    quads = layers // shards
    buckets = 2 * places
    core = lax.axis_index("query")
    layer = lax.axis_index("lib") // 4

    def send(value, first, second):
        pairs = [
            (c * places + i, c * places + (i ^ (second if c % 2 else first)))
            for c in range(shards)
            for i in range(places)
        ]
        return lax.ppermute(value, ("query", "lib"), pairs)

    def layer_pairs(stream, distance):
        for s in range(shards):
            for i in range(places):
                worker, at = divmod(i // 4, quads)
                yield (s ^ distance) * places + i, worker * places + ((at ^ stream) + quads * s) * 4 + i % 4

    def spread(value, stream):
        return lax.ppermute(value, ("query", "lib"), list(layer_pairs(stream, 0)))

    def collect(value, stream, distance):
        return lax.ppermute(value, ("query", "lib"), [(b, a) for a, b in layer_pairs(stream, distance)])

    def swap(value, distance):
        return lax.ppermute(value, "query", [(c, c ^ distance) for c in range(shards)])

    blocks = 3
    own = pack(
        [queries] + [swap(queries, d) for d in range(1, shards)],
        [query_bucket] + [swap(query_bucket, d) for d in range(1, shards)],
    )

    tie = lax.optimization_barrier
    near = [spread(own, at) for at in range(quads)]
    entries, firsts = sort_library(blocks, buckets, library, library_time, library_bucket)
    entries, firsts, near = tie((entries, firsts, near))
    libraries = [entries] + [swap(entries, d) for d in range(1, shards)]
    firsts = firsts[:, 0]
    firsts = jnp.concatenate([firsts] + [swap(firsts, d) for d in range(1, shards)])
    second = [send(n, 2, 1) for n in near]
    second, near = tie((second, near))
    wide = [jnp.concatenate(both, axis=0) for both in zip(near, second)]

    far = [send(w, 1, 2) for w in wide]
    quad = jnp.stack([core * quads + (at ^ (layer % quads)) for at in range(quads)]).astype(jnp.int32)
    matched = match_near(quad, firsts, near, second, libraries, per_bucket, blocks, buckets)
    from_second = [send(second_sums, 2, 1) for _, _, _, second_sums in matched]
    far, matched = tie((far, matched))
    first_sums, from_corner = [], []
    for at, (held, facts, _, _) in enumerate(matched):
        sums, corner_sums = match_far(far[at], held, facts)
        first_sums.append(sums)
        from_corner.append(send(corner_sums, 2, 1))
    returned = []
    for at, (_, _, near_sums, _) in enumerate(matched):
        if at == 0:
            first_sums[0], from_second = tie((first_sums[0], from_second))
        (sums,) = merge([first_sums[at], from_corner[at]], 1)
        pieces = merge([near_sums, from_second[at], send(sums, 1, 2)], shards)
        returned += [collect(piece, at, d) for d, piece in enumerate(pieces)]
    return finish(returned)


def solution(mesh):
    placed = (
        P(("query", "lib"), None),
        P(("query", "lib")),
        P(("lib", "query"), None),
        P(("lib", "query")),
        P(("lib", "query")),
    )
    return jax.shard_map(
        functools.partial(per_device, mesh.shape["query"], mesh.shape["lib"]),
        mesh=mesh,
        in_specs=placed,
        out_specs=(P(("query", "lib"), None), P(("query", "lib")), P(("query", "lib"))),
        check_vma=False,
    )
```

```python
import functools
import math

import jax
import jax.numpy as jnp
from jax import lax
from jax.experimental import pallas as pl
from jax.experimental.pallas import tpu as pltpu
from jax.sharding import PartitionSpec as P

SHARPNESS = 448
EPSILON = 1e-06
LANES = 128
LOG2E = math.log2(math.e)
LN2 = math.log(2.0)
FRACTION_BITS = 14
SUM_BITS = 16
LOW_BITS = 15
MASKED = -1e30
OUTSIDE = 1e6
UNIT = 16
LARGEST = 8
SORT_MIB, MATCH_MIB, MERGE_MIB = 20, 20, 4
NT = (((1,), (1,)), ((), ()))
MIB = 1 << 20


def in_place(*arrays):
    return [pltpu.with_memory_space_constraint(a, pltpu.HBM) for a in arrays]


def split3(value):
    pieces = []
    for _ in range(3):
        piece = value.astype(jnp.bfloat16)
        pieces.append(piece)
        value = value - piece.astype(jnp.float32)
    return pieces


def sort_kernel(buckets, time_ref, bucket_ref, library_ref, sorted_ref, first_ref, times, bucket_ids, facts_ref, held, arrived):
    step = pl.program_id(0)
    total, bins = held.shape
    count = sorted_ref.shape[0]
    small = [
        pltpu.make_async_copy(time_ref, times, arrived.at[0]),
        pltpu.make_async_copy(bucket_ref, bucket_ids, arrived.at[1]),
    ]

    def block(n):
        rows = pl.ds(pl.multiple_of(n * count, UNIT), count)
        return pltpu.make_async_copy(library_ref.at[rows, :], held.at[rows, :], arrived.at[2 + n])

    @pl.when(step == 0)
    def _():
        for c in small + [block(n) for n in range(total // count)]:
            c.start()
        for c in small:
            c.wait()
        facts_ref[0:1, :] = times[...].astype(jnp.float32).reshape(1, total)
        facts_ref[1:2, :] = bucket_ids[...].astype(jnp.float32).reshape(1, total)

    def earlier(n):
        order = [lax.broadcasted_iota(jnp.int32, (n, n), d) for d in range(2)]
        return (order[0] < order[1]).astype(jnp.float32).astype(jnp.bfloat16)

    here = pl.ds(pl.multiple_of(pl.program_id(0) * count, LANES), count)
    time, bucket = facts_ref[0:1, here], facts_ref[1:2, here]
    member = (
        bucket == lax.broadcasted_iota(jnp.int32, (buckets, count), 0).astype(jnp.float32)
    ).astype(jnp.float32)
    member16 = member.astype(jnp.bfloat16)
    before = jnp.dot(member16, earlier(count), preferred_element_type=jnp.float32)
    lower = lax.dot_general(
        earlier(buckets), member16, (((0,), (0,)), ((), ())), preferred_element_type=jnp.float32
    )
    first = jnp.sum(lower, axis=1, keepdims=True)
    place = jnp.sum(member * (before + first), axis=0, keepdims=True).astype(jnp.int32)
    first_ref[...] = jnp.broadcast_to(first, (buckets, LANES)).astype(jnp.int32)
    chosen = (
        (lax.broadcasted_iota(jnp.int32, (count, count), 0) == place)
        .astype(jnp.float32)
        .astype(jnp.bfloat16)
    )

    block(step).wait()
    entries = held[pl.ds(pl.multiple_of(step * count, UNIT), count), :]
    wide = entries.astype(jnp.float32)
    scale = lax.rsqrt(jnp.sum(wide * wide, axis=1, keepdims=True) / bins + EPSILON)
    which = lax.broadcasted_iota(jnp.int32, (LANES, count), 0)
    facts = jnp.where(which == 0, time, jnp.where(which == 1, bucket, 0.0)).T
    lane = lax.broadcasted_iota(jnp.int32, (count, LANES), 1)
    for at, piece in enumerate(split3(scale)):
        facts = jnp.where(lane == 2 + at, piece.astype(jnp.float32), facts)
    sorted_ref[:, :bins] = jnp.dot(chosen, entries, preferred_element_type=jnp.float32).astype(
        jnp.bfloat16
    )
    sorted_ref[:, bins:] = jnp.dot(
        chosen, facts.astype(jnp.bfloat16), preferred_element_type=jnp.float32
    ).astype(jnp.bfloat16)


def sort_library(blocks, buckets, library, library_time, library_bucket):
    total, bins = library.shape
    count = total // blocks
    return pl.pallas_call(
        functools.partial(sort_kernel, buckets),
        out_shape=(
            jax.ShapeDtypeStruct((total, bins + LANES), jnp.bfloat16),
            jax.ShapeDtypeStruct((blocks * buckets, LANES), jnp.int32),
        ),
        grid=(blocks,),
        in_specs=[pl.BlockSpec(memory_space=pltpu.HBM)] * 3,
        out_specs=[
            pl.BlockSpec((count, bins + LANES), lambda n: (n, 0)),
            pl.BlockSpec((buckets, LANES), lambda n: (n, 0)),
        ],
        scratch_shapes=[
            pltpu.VMEM((total,), library_time.dtype),
            pltpu.VMEM((total,), library_bucket.dtype),
            pltpu.VMEM((8, total), jnp.float32),
            pltpu.VMEM((total, bins), library.dtype),
            pltpu.SemaphoreType.DMA((2 + blocks,)),
        ],
        compiler_params=pltpu.CompilerParams(vmem_limit_bytes=SORT_MIB * MIB),
        cost_estimate=pl.CostEstimate(flops=5 * count * total * bins, bytes_accessed=4 * total * bins, transcendentals=0),
        name="sort_library",
    )(*in_place(library_time, library_bucket, library))


def encode(out, rows, vector, k, total, time_sum):
    bins = vector.shape[1]
    largest = jnp.maximum(jnp.max(jnp.abs(vector), axis=1, keepdims=True), 1e-30)
    e = jnp.ceil(jnp.log2(largest))
    coded = jnp.floor(vector * jnp.exp2(FRACTION_BITS - e) + 0.5).astype(jnp.int32)
    out[rows, :bins] = coded.astype(jnp.int16)
    lane = lax.broadcasted_iota(jnp.int32, (vector.shape[0], LANES), 1)
    total = (total * (1 << SUM_BITS) + 0.5).astype(jnp.int32)
    time_sum = (time_sum * (1 << SUM_BITS) + 0.5).astype(jnp.int32)
    low = (1 << LOW_BITS) - 1
    stats = jnp.zeros((vector.shape[0], LANES), jnp.int32)
    for at, value in enumerate(
        (k.astype(jnp.int32), e.astype(jnp.int32), total >> LOW_BITS, total & low, time_sum >> LOW_BITS, time_sum & low)
    ):
        stats = jnp.where(lane == at, value, stats)
    out[rows, bins:] = stats.astype(jnp.int16)


def merged(parts):
    bins = parts[0].shape[1] - LANES
    stats = [p[:, bins:].astype(jnp.int32).astype(jnp.float32) for p in parts]
    ks = [s[:, 0:1] for s in stats]
    k = functools.reduce(jnp.maximum, ks)
    high = float(1 << LOW_BITS)
    unit = 1.0 / (1 << SUM_BITS)
    vector = total = time_sum = 0.0
    for part, s, own in zip(parts, stats, ks):
        shift = jnp.exp2(own - k)
        total = total + (s[:, 2:3] * high + s[:, 3:4]) * (shift * unit)
        time_sum = time_sum + (s[:, 4:5] * high + s[:, 5:6]) * (shift * unit)
        factor = jnp.exp2(own - k + s[:, 1:2] - FRACTION_BITS)
        vector = vector + part[:, :bins].astype(jnp.int32).astype(jnp.float32) * factor
    return vector, k, total, time_sum


def merge_kernel(pieces, *refs):
    parts = refs[: len(refs) - pieces]
    outs = refs[len(refs) - pieces :]
    rows = parts[0].shape[0] // pieces
    for at, out in enumerate(outs):
        own = [p[at * rows : (at + 1) * rows, :] for p in parts]
        encode(out, slice(None), *merged(own))


def merge(parts, pieces):
    rows, width = parts[0].shape
    out = jax.ShapeDtypeStruct((rows // pieces, width), jnp.int16)
    return pl.pallas_call(
        functools.partial(merge_kernel, pieces),
        out_shape=(out,) * pieces,
        compiler_params=pltpu.CompilerParams(vmem_limit_bytes=MERGE_MIB * MIB),
        cost_estimate=pl.CostEstimate(flops=8 * rows * width * len(parts), bytes_accessed=2 * rows * width * (len(parts) + 1), transcendentals=0),
        name="merge",
    )(*parts)


def finish_kernel(*refs):
    *parts, spectra_ref, time_ref, evidence_ref = refs
    vector, k, total, time_sum = merged([p[...] for p in parts])
    spectra_ref[...] = (vector / total).astype(jnp.bfloat16)
    shape = (total.shape[0], LANES)
    time_ref[...] = jnp.broadcast_to(time_sum / total, shape).T[:1]
    evidence_ref[...] = jnp.broadcast_to(k * LN2 + jnp.log(total), shape).T[:1]


def finish(parts):
    rows, width = parts[0].shape
    spectra, time, evidence = pl.pallas_call(
        finish_kernel,
        out_shape=(
            jax.ShapeDtypeStruct((rows, width - LANES), jnp.bfloat16),
            jax.ShapeDtypeStruct((1, rows), jnp.float32),
            jax.ShapeDtypeStruct((1, rows), jnp.float32),
        ),
        compiler_params=pltpu.CompilerParams(vmem_limit_bytes=MERGE_MIB * MIB),
        name="finish",
    )(*parts)
    return spectra, time.reshape(rows), evidence.reshape(rows)


def pack_kernel(*refs):
    *parts, out = refs
    count = len(parts) // 2
    rows, bins = parts[0].shape
    for d in range(count):
        at = slice(d * rows, (d + 1) * rows)
        out[at, :bins] = parts[d][...]
        bucket = parts[count + d][...].reshape(1, rows).astype(jnp.float32)
        if rows < LANES:
            bucket = jnp.concatenate([bucket, jnp.zeros((1, LANES - rows), jnp.float32)], axis=1)
        columns = jnp.broadcast_to(bucket, (LANES, LANES)).T
        out[at, bins:] = columns[:rows].astype(jnp.bfloat16)


def pack(queries, buckets):
    rows, bins = queries[0].shape
    return pl.pallas_call(
        pack_kernel,
        out_shape=jax.ShapeDtypeStruct((len(queries) * rows, bins + LANES), jnp.bfloat16),
        compiler_params=pltpu.CompilerParams(vmem_limit_bytes=MERGE_MIB * MIB),
        name="pack",
    )(*queries, *buckets)


def window_kernel(shards, blocks, buckets, quad_ref, first_ref, *refs):
    libraries, refs, arrived = refs[:shards], refs[shards:-1], refs[-1]
    nears, seconds, helds, factses, *parts = (refs[at :: 6] for at in range(6))
    count = libraries[0].shape[0] // blocks
    entries, width = helds[0].shape
    share = entries // shards

    def fetch(held, sem, library, begin, units, filled):
        def copy(size, done):
            pltpu.make_async_copy(
                library.at[pl.ds(pl.multiple_of((begin + done) * UNIT, UNIT), size * UNIT), :],
                held.at[pl.ds(pl.multiple_of((filled + done) * UNIT, UNIT), size * UNIT), :],
                sem,
            ).start()

        most = LARGEST
        while most * UNIT > count:
            most //= 2

        def large(i, carry):
            copy(most, i * most)
            return carry

        lax.fori_loop(0, units // most, large, 0)
        size = most // 2
        while size:

            @pl.when((units & size) != 0)
            def _(size=size):
                copy(size, units // (2 * size) * (2 * size))

            size //= 2

    filled = []
    for at, held in enumerate(helds):
        low = jnp.maximum(8 * quad_ref[at] - 1, 0)
        high = 8 * quad_ref[at] + 9
        for shard, library in enumerate(libraries):
            region, sem = held.at[shard * share : (shard + 1) * share, :], arrived.at[at, shard]
            there = jnp.int32(0)
            for n in range(blocks):
                row = (shard * blocks + n) * buckets
                start = first_ref[row + low]
                end = first_ref[row + jnp.minimum(high, buckets - 1)]
                end = jnp.where(high >= buckets, count, end)
                begin = start // UNIT
                units = (end + UNIT - 1) // UNIT - begin
                fetch(region, sem, library, n * (count // UNIT) + begin, units, there)
                there = there + units
            fetch(region, sem, library, 0, share // UNIT - there, there)
            filled.append(there)

    for at, held in enumerate(helds):
        queries = jnp.concatenate([nears[at][...], seconds[at][...]], axis=0)
        products, here = [], []
        for shard in range(shards):
            region = held.at[shard * share : (shard + 1) * share, :]
            pltpu.make_async_copy(region, region, arrived.at[at, shard]).wait()
            products.append(score(queries, region))
            row = lax.broadcasted_iota(jnp.int32, (1, share), 1)
            here.append(row - filled[at * shards + shard] * UNIT)
        columns = held[:, width - LANES :].astype(jnp.float32).T
        which = lax.broadcasted_iota(jnp.int32, (8, entries), 0)
        bucket = jnp.where(jnp.concatenate(here, axis=1) < 0, columns[1:2], OUTSIDE)
        scale = columns[2:3] + columns[3:4] + columns[4:5]
        facts = jnp.where(which == 0, columns[0:1], jnp.where(which == 1, bucket, scale))
        factses[at][...] = facts
        weigh(queries, jnp.concatenate(products, axis=1), facts, held, [p[at] for p in parts])


def rest_kernel(far_ref, held, facts_ref, *parts):
    queries = far_ref[...]
    weigh(queries, score(queries, held), facts_ref[...], held, parts)


def score(queries, held):
    bins = queries.shape[1] - LANES
    return lax.dot_general(
        queries[:, :bins], held[:, :bins], NT, preferred_element_type=jnp.float32
    )


def weigh(queries, products, facts, held, parts):
    rows, width = queries.shape
    bins = width - LANES
    wide = queries[:, :bins].astype(jnp.float32)
    mean = jnp.sum(wide * wide, axis=1, keepdims=True) / bins
    query_scale = lax.rsqrt(mean + EPSILON) * (SHARPNESS / bins)
    query_bucket = queries[:, bins:].astype(jnp.float32)[:, 0:1]
    time, bucket, scale = facts[0:1], facts[1:2], facts[2:3]
    scores = products * query_scale * scale * LOG2E
    scores = jnp.where(jnp.abs(query_bucket - bucket) <= 1.0, scores, MASKED)
    k = jnp.ceil(jnp.max(scores, axis=1, keepdims=True))
    weights = jnp.exp2(scores - k)
    total = jnp.sum(weights, axis=1, keepdims=True)
    time_sum = jnp.sum(weights * time, axis=1, keepdims=True)
    upper = weights.astype(jnp.bfloat16)
    lower = (weights - upper.astype(jnp.float32)).astype(jnp.bfloat16)
    both = jnp.concatenate([upper, lower], axis=0)
    sums = jnp.dot(both, held[:, :bins], preferred_element_type=jnp.float32)
    vector = sums[:rows] + sums[rows:]
    for n, part in enumerate(parts):
        at = slice(n * rows // len(parts), (n + 1) * rows // len(parts))
        encode(part, slice(None), vector[at], k[at], total[at], time_sum[at])


def match_near(quad, firsts, near, second, libraries, per_bucket, blocks, buckets):
    quads = len(near)
    rows, width = near[0].shape
    bins = width - LANES
    shards = len(libraries)
    units = (10 * per_bucket + blocks * 2 * (UNIT - 1)) // UNIT
    entries = shards * (-(-units * UNIT // LANES) * LANES)
    vmem, smem = pl.BlockSpec(memory_space=pltpu.VMEM), pl.BlockSpec(memory_space=pltpu.SMEM)
    outs = (
        jax.ShapeDtypeStruct((entries, width), jnp.bfloat16),
        jax.ShapeDtypeStruct((8, entries), jnp.float32),
        jax.ShapeDtypeStruct((rows, width), jnp.int16),
        jax.ShapeDtypeStruct((rows, width), jnp.int16),
    )

    def kernel(quad_ref, first_ref, *refs):
        ins, rest = refs[: shards + 2 * quads], refs[shards + 2 * quads :]
        by_quad = []
        for at in range(quads):
            by_quad += ins[shards + 2 * at : shards + 2 * at + 2]
            by_quad += rest[4 * at : 4 * at + 4]
        window_kernel(shards, blocks, buckets, quad_ref, first_ref, *ins[:shards], *by_quad, rest[-1])

    results = pl.pallas_call(
        kernel,
        out_shape=outs * quads,
        in_specs=[smem, smem] + [pl.BlockSpec(memory_space=pl.ANY)] * shards + [vmem] * (2 * quads),
        out_specs=[vmem] * (4 * quads),
        scratch_shapes=[pltpu.SemaphoreType.DMA((quads, shards))],
        compiler_params=pltpu.CompilerParams(vmem_limit_bytes=MATCH_MIB * MIB),
        cost_estimate=pl.CostEstimate(
            flops=45 * quads * rows * entries * bins, bytes_accessed=2 * entries * width, transcendentals=0
        ),
        name="match_near",
    )(quad, firsts, *libraries, *[q for both in zip(near, second) for q in both])
    return [results[4 * at : 4 * at + 4] for at in range(quads)]


def match_far(far, held, facts):
    rows, width = far.shape
    return pl.pallas_call(
        rest_kernel,
        out_shape=(jax.ShapeDtypeStruct((rows // 2, width), jnp.int16),) * 2,
        compiler_params=pltpu.CompilerParams(vmem_limit_bytes=MATCH_MIB * MIB),
        cost_estimate=pl.CostEstimate(flops=15 * rows * held.shape[0] * width, bytes_accessed=2 * held.size, transcendentals=0),
        name="match_far",
    )(far, held, facts)


def per_device(shards, places, queries, query_bucket, library, library_time, library_bucket):
    own_rows, bins = queries.shape
    per_bucket = library.shape[0] // (2 * places)
    layers = places // 4
    quads = layers // shards
    buckets = 2 * places
    core = lax.axis_index("query")
    layer = lax.axis_index("lib") // 4

    def send(value, first, second):
        pairs = [
            (c * places + i, c * places + (i ^ (second if c % 2 else first)))
            for c in range(shards)
            for i in range(places)
        ]
        return lax.ppermute(value, ("query", "lib"), pairs)

    def layer_pairs(stream, distance):
        for s in range(shards):
            for i in range(places):
                worker, at = divmod(i // 4, quads)
                yield (s ^ distance) * places + i, worker * places + ((at ^ stream) + quads * s) * 4 + i % 4

    def spread(value, stream):
        return lax.ppermute(value, ("query", "lib"), list(layer_pairs(stream, 0)))

    def collect(value, stream, distance):
        return lax.ppermute(value, ("query", "lib"), [(b, a) for a, b in layer_pairs(stream, distance)])

    def swap(value, distance):
        return lax.ppermute(value, "query", [(c, c ^ distance) for c in range(shards)])

    blocks = 3
    own = pack(
        [queries] + [swap(queries, d) for d in range(1, shards)],
        [query_bucket] + [swap(query_bucket, d) for d in range(1, shards)],
    )

    tie = lax.optimization_barrier
    near = [spread(own, at) for at in range(quads)]
    entries, firsts = sort_library(blocks, buckets, library, library_time, library_bucket)
    entries, firsts, near = tie((entries, firsts, near))
    libraries = [entries] + [swap(entries, d) for d in range(1, shards)]
    firsts = firsts[:, 0]
    firsts = jnp.concatenate([firsts] + [swap(firsts, d) for d in range(1, shards)])
    second = [send(n, 2, 1) for n in near]
    second, near = tie((second, near))
    wide = [jnp.concatenate(both, axis=0) for both in zip(near, second)]

    far = [send(w, 1, 2) for w in wide]
    quad = jnp.stack([core * quads + (at ^ (layer % quads)) for at in range(quads)]).astype(jnp.int32)
    matched = match_near(quad, firsts, near, second, libraries, per_bucket, blocks, buckets)
    from_second = [send(second_sums, 2, 1) for _, _, _, second_sums in matched]
    far, matched = tie((far, matched))
    first_sums, from_corner = [], []
    for at, (held, facts, _, _) in enumerate(matched):
        sums, corner_sums = match_far(far[at], held, facts)
        first_sums.append(sums)
        from_corner.append(send(corner_sums, 2, 1))
    returned = []
    for at, (_, _, near_sums, _) in enumerate(matched):
        if at == 0:
            first_sums[0], from_second = tie((first_sums[0], from_second))
        (sums,) = merge([first_sums[at], from_corner[at]], 1)
        pieces = merge([near_sums, from_second[at], send(sums, 1, 2)], shards)
        returned += [collect(piece, at, d) for d, piece in enumerate(pieces)]
    return finish(returned)


def solution(mesh):
    placed = (
        P(("query", "lib"), None),
        P(("query", "lib")),
        P(("lib", "query"), None),
        P(("lib", "query")),
        P(("lib", "query")),
    )
    return jax.shard_map(
        functools.partial(per_device, mesh.shape["query"], mesh.shape["lib"]),
        mesh=mesh,
        in_specs=placed,
        out_specs=(P(("query", "lib"), None), P(("query", "lib")), P(("query", "lib"))),
        check_vma=False,
    )
```
